32 devices in a mesh: chan: 8 (over z, y), sky: 4 (over x, core).
Axes of the slice: x: 2, y: 2, z: 4, core: 2. Of those that a mesh axis runs over, the one named last changes fastest.
Arguments:
- sky_map: float32 [1024, 16384], P('chan', 'sky')
- templates: float32 [1024, 30], replicated, may hold values from -6 to 6
- noise_var: float32 [1024], replicated, may hold values from 0.5 to 2
- block_order: int32 [4, 32], P('sky'), may hold values from 0 to 31, each once within a row
- patch_count: int32 [4, 8], P('sky'), may hold values from 1 to 8, as said below
- slab_dest: int32 [4, 8, 8], P('sky'), may hold values from 0 to 3, as said below
Outputs:
- slab_cube: float32 [1024, 256, 128], P('chan', 'sky')
The draws below stay inside these ranges and needn't reach their ends.
Inputs may be any that keep to these rules, and one draw needn't show every extreme that they name: `slab_dest`: taken in order of owners and then slots, the live slots of a sky group (slots below the owner's count) cycle through all 4 slabs in one fixed order, so every slab gets exactly 8 live slots of each group and no owner names a slab more than 2 times; slots at or beyond the owner's count are ignored. `patch_count`: in each sky group the counts sum to 32 and the largest is 8. `block_order`: each row is an ordering of the group's 32 blocks.
All inputs are finite; a program needn't handle non-finite values.
Results may differ from the reference program's by a relative error of at most 0.0003.
Values sent between devices are 32-bit elements; how exact they have to be, the bound alone decides.
No kernel may reach another device: no remote copies, remote signals or barrier semaphores. Data moves between devices by JAX's collectives and lax.ppermute only.
A program may use at most 64 MiB of HBM per device.

```python
import math
import jax
import jax.numpy as jnp
from jax import lax

NU = 1024
NT = 30
BLK = 128
BPO = 4
CAP = 8
DCAP = 2
NB_G = 32
PIX = 16384
SLAB_ROWS = 64
N_CHAN = 8
N_SKY = 4


def draw_sky_map(key, part):
    key_chan, key_pixel, key_base, key_spectra, key_strength = jax.random.split(jax.random.fold_in(key, 11), 5)
    chan_scale = jnp.exp(jax.random.uniform(key_chan, (NU, 1), jnp.float32, math.log(0.3), math.log(3.0)))
    pixel_scale = jnp.exp(jax.random.uniform(key_pixel, (1, PIX), jnp.float32, math.log(0.1), math.log(10.0)))
    spectra = jax.random.normal(key_spectra, (NU, 6), jnp.float32)
    strengths = jax.random.normal(key_strength, (6, PIX), jnp.float32)
    field_sum = jax.random.normal(key_base, (NU, PIX), jnp.float32)
    gain_low = 0.3
    gain_high = 1.2
    for mode_index in range(6):
        gain_value = gain_low * (gain_high / gain_low) ** (mode_index / 5.0)
        field_sum = field_sum + gain_value * spectra[:, mode_index:mode_index + 1] * strengths[mode_index:mode_index + 1, :]
    return (field_sum * chan_scale * pixel_scale).astype(jnp.float32)


def group_counts(group_key):
    key_perm, key_pair = jax.random.split(group_key, 2)
    order = jax.random.permutation(key_perm, N_CHAN)
    rank = jnp.arange(N_CHAN, dtype=jnp.int32)
    pair_index = jnp.maximum(rank - 3, 0) // 2
    sign_value = jnp.where((rank - 3) % 2 == 0, 1, -1)
    has_partner = (rank >= 3) & (pair_index * 2 + 4 < N_CHAN)
    shifts = jax.random.randint(key_pair, (N_CHAN,), -(BPO - 1), BPO)
    by_rank = BPO + jnp.where(has_partner, sign_value * jnp.take(shifts, pair_index), 0)
    by_rank = jnp.where(rank == 0, CAP, by_rank)
    by_rank = jnp.where(rank == 1, 1, by_rank)
    by_rank = jnp.where(rank == 2, BPO - 1, by_rank)
    return jnp.zeros((N_CHAN,), jnp.int32).at[order].set(by_rank.astype(jnp.int32))


def shared_counts(key):
    group_keys = jax.random.split(jax.random.fold_in(key, 31), N_SKY)
    return jax.vmap(group_counts)(group_keys).astype(jnp.int32)


def draw_patch_count(key, part):
    return shared_counts(key)


def draw_slab_dest(key, part):
    counts = shared_counts(key)
    group_keys = jax.random.split(jax.random.fold_in(key, 37), N_SKY)

    def one_group(group_key, counts_row):
        key_shift, key_label = jax.random.split(group_key, 2)
        shift = jax.random.randint(key_shift, (), 0, N_SKY)
        labels = jax.random.permutation(key_label, N_SKY).astype(jnp.int32)
        offsets = jnp.cumsum(counts_row) - counts_row
        slot_index = jnp.arange(CAP, dtype=jnp.int32)
        position = offsets[:, None] + slot_index[None, :]
        live = jnp.take(labels, (position + shift) % N_SKY)
        return jnp.where(slot_index[None, :] < counts_row[:, None], live, slot_index[None, :] % N_SKY)
    return jax.vmap(one_group)(group_keys, counts).astype(jnp.int32)


def bell_draw(own_key, extent, width, reach, held_as=jnp.bfloat16):
    array = width * jax.random.normal(own_key, extent, jnp.float32)
    return jnp.clip(array, min=-reach, max=reach).astype(held_as)


def setup_inputs(seed: int = 0) -> dict:
    key_of = jax.random.split(jax.random.key(seed), 7)
    return {
        "sky_map": draw_sky_map(jax.random.fold_in(key_of[6], 71), 0),
        "templates": bell_draw(key_of[1], (NU, NT), 1.0, 6.0, jnp.float32),
        "noise_var": jnp.clip(jnp.exp(jax.random.uniform(key_of[2], (NU,), jnp.float32, math.log(0.5), math.log(2.0))), 0.5, 2.0),
        "block_order": jax.vmap(lambda own: jax.random.permutation(own, NB_G))(jax.random.split(key_of[3], N_SKY)).reshape((N_SKY, NB_G)).astype(jnp.int32),
        "patch_count": draw_patch_count(jax.random.fold_in(key_of[6], 71), 0),
        "slab_dest": draw_slab_dest(jax.random.fold_in(key_of[6], 71), 0),
    }


def owner_blocks(order_row, counts_row):
    offsets = jnp.cumsum(counts_row) - counts_row
    slot_index = jnp.arange(CAP, dtype=jnp.int32)
    live_slots = slot_index[None, :] < counts_row[:, None]
    position = jnp.where(live_slots, offsets[:, None] + slot_index[None, :], 0).astype(jnp.int32)
    return (jnp.take(order_row, position, axis=0), live_slots)

def slab_sources(dest_row, block_count, sky_count, slab_cap):
    slot_index = jnp.arange(dest_row.shape[0], dtype=jnp.int32)
    live_slots = slot_index < block_count
    earlier = (dest_row[:, None] == dest_row[None, :]) & live_slots[:, None] & live_slots[None, :] & (slot_index[None, :] < slot_index[:, None])
    rank_in_slab = jnp.sum(earlier.astype(jnp.int32), axis=1)
    target_row = dest_row * slab_cap + rank_in_slab
    row_index = jnp.arange(sky_count * slab_cap, dtype=jnp.int32)
    matches = (target_row[None, :] == row_index[:, None]) & live_slots[None, :]
    source_slot = jnp.sum(jnp.where(matches, slot_index[None, :], 0), axis=1).astype(jnp.int32)
    return (source_slot, jnp.any(matches, axis=1))

def template_amplitudes(pixels, block_count, templates, noise_var):
    highest = lax.Precision.HIGHEST
    covariance = jnp.dot(pixels, pixels.T, precision=highest) / (block_count * BLK).astype(jnp.float32) + jnp.diag(noise_var)
    factor = jnp.linalg.cholesky(covariance)
    weighted = jax.scipy.linalg.cho_solve((factor, True), templates)
    gram_matrix = jnp.dot(templates.T, weighted, precision=highest)
    projected = jnp.dot(weighted.T, pixels, precision=highest)
    return jax.scipy.linalg.cho_solve((jnp.linalg.cholesky(gram_matrix), True), projected)

def reference(sky_map, templates, noise_var, block_order, patch_count, slab_dest):
    group_cube = sky_map.reshape(NU, N_SKY, NB_G, BLK)

    def one_owner(owner_index):
        group_index = owner_index // N_CHAN
        member = owner_index % N_CHAN
        blocks, live_slots = owner_blocks(block_order[group_index], patch_count[group_index])
        own_blocks = blocks[member]
        own_live = live_slots[member]
        block_count = patch_count[group_index, member]
        group_part = lax.dynamic_index_in_dim(group_cube, group_index, 1, keepdims=False)
        pixels = jnp.take(group_part, own_blocks, axis=1)
        pixels = jnp.where(own_live[None, :, None], pixels, 0.0).reshape(NU, CAP * BLK)
        amplitudes = template_amplitudes(pixels, block_count, templates, noise_var)
        cleaned = pixels - jnp.dot(templates, amplitudes, precision=lax.Precision.HIGHEST)
        source_slot, filled = slab_sources(slab_dest[group_index, member], block_count, N_SKY, DCAP)
        slab_block = jnp.take(cleaned.reshape(NU, CAP, BLK), source_slot, axis=1)
        return jnp.where(filled[None, :, None], slab_block, 0.0)
    owners = lax.map(one_owner, jnp.arange(N_SKY * N_CHAN, dtype=jnp.int32))
    owners = owners.reshape(N_SKY, N_CHAN, NU, N_SKY, DCAP, BLK)
    return jnp.transpose(owners, (2, 3, 0, 1, 4, 5)).reshape(NU, N_SKY * SLAB_ROWS, BLK)
```

```python
import functools

import jax
import jax.numpy as jnp
from jax import lax
from jax.experimental import pallas as pl
from jax.experimental.pallas import tpu as pltpu
from jax.sharding import PartitionSpec as P

BLK = 128
CAP = 8
TPAD = 32
STEP = 128
HIGHEST = lax.Precision.HIGHEST
F32 = jnp.float32
ANY = pl.BlockSpec(memory_space=pl.ANY)
SMEM = pl.BlockSpec(memory_space=pltpu.SMEM)
VMEM = pl.BlockSpec(memory_space=pltpu.VMEM)
PARAMS = pltpu.CompilerParams(vmem_limit_bytes=48 * 1024 * 1024)


def dot(a, b, contract):
    return lax.dot_general(
        a, b, (contract, ((), ())), precision=HIGHEST, preferred_element_type=F32
    )


def reciprocal(value):
    guess = pl.reciprocal(value, approx=True)
    guess = guess * (2.0 - value * guess)
    return guess * (2.0 - value * guess)


def panel_factor(groups, first):
    lane = lax.broadcasted_iota(jnp.int32, (8, BLK), 1)
    sub = lax.broadcasted_iota(jnp.int32, (8, BLK), 0)
    spread = lambda v, i: jnp.broadcast_to(v[i : i + 1, :], (8, BLK))
    groups = list(groups)
    count = len(groups)
    done = []
    for g in range(count):
        k = first + 8 * g
        cols = [
            [jnp.broadcast_to(groups[i][:, k + j : k + j + 1], (8, BLK)) for j in range(8)]
            for i in range(g, count)
        ]
        pivots = (lane >= k) & (lane < k + 8)
        unit = jnp.where(pivots, jnp.where(lane - k == sub, 1.0, 0.0), groups[g])
        entry = {(a, b): spread(cols[0][b], a) for a in range(8) for b in range(a + 1)}
        rows = [spread(unit, j) for j in range(8)]
        inverse = []
        lower = {}
        for j in range(8):
            inverse.append(reciprocal(entry[j, j]))
            for a in range(j + 1, 8):
                lower[a, j] = entry[a, j] * inverse[j]
            for a in range(j + 1, 8):
                for b in range(j + 1, a + 1):
                    entry[a, b] = entry[a, b] - lower[a, j] * entry[b, j]
                rows[a] = rows[a] - lower[a, j] * rows[j]
        done.append(
            jnp.concatenate([(rows[j] * lax.rsqrt(entry[j, j]))[0:1] for j in range(8)], axis=0)
        )
        if g + 1 == count:
            break
        solved = [None] * 8
        for j in reversed(range(8)):
            value = rows[j] * inverse[j]
            for m in range(j + 1, 8):
                value = value - lower[m, j] * solved[m]
            solved[j] = value
        for i in range(g + 1, count):
            terms = [cols[i - g][j] * solved[j] for j in range(8)]
            while len(terms) > 1:
                terms = [terms[q] + terms[q + 1] for q in range(0, len(terms), 2)]
            groups[i] = jnp.where(pivots, 0.0, groups[i]) - terms[0]
    return jnp.concatenate(done, axis=0)


def inverse_factor(matrix):
    wide = 32
    lane = lax.broadcasted_iota(jnp.int32, (wide, BLK), 1)
    row = lax.broadcasted_iota(jnp.int32, (wide, BLK), 0)
    groups = [matrix[8 * g : 8 * g + 8, :] for g in range(BLK // 8)]
    out = []
    for first in range(0, BLK, wide):
        last = first + wide
        panel = panel_factor(groups[first // 8 : last // 8], first)
        out.append(jnp.where(lane <= row + first, panel, 0.0))
        if last == BLK:
            break
        kept = jnp.where((lane <= row + first) | (lane >= last), panel, 0.0)
        update = dot(kept, kept, ((0,), (0,)))
        lane8 = lax.broadcasted_iota(jnp.int32, (8, BLK), 1)
        inside = (lane8 >= first) & (lane8 < last)
        for i in range(last // 8, BLK // 8):
            groups[i] = jnp.where(inside, 0.0, groups[i]) - update[8 * i : 8 * i + 8, :]
    return jnp.concatenate(out, axis=0)


def chan_pack_kernel(chans, blocks, rows, me_ref, order_ref, count_ref, map_ref, *rest):
    outs, (held, start, sem_in, sem) = rest[:chans], rest[chans:]
    load = pltpu.make_async_copy(map_ref, held.at[:, : blocks * BLK], sem_in)
    load.start()
    held[:, blocks * BLK :] = jnp.zeros((rows, BLK), F32)
    total = jnp.int32(0)
    for c in range(chans):
        start[c] = total
        total = total + count_ref[0, c]
    load.wait()
    for p in reversed(range(chans)):
        owner = me_ref[0] ^ p
        offset = start[owner]
        live = count_ref[0, owner]
        for j in range(CAP):
            place = jnp.minimum(offset + j, blocks - 1)
            block = jnp.where(j < live, order_ref[0, place], blocks)
            pltpu.make_async_copy(
                held.at[:, pl.ds(pl.multiple_of(block * BLK, BLK), BLK)],
                outs[p].at[:, j * BLK : (j + 1) * BLK],
                sem.at[p],
            ).start()
    for p in range(chans):
        pltpu.make_async_copy(held.at[:, : CAP * BLK], outs[p], sem.at[p]).wait()


def sky_pack_kernel(chans, skies, cap, blocks, rows, me_ref, order_ref, count_ref, dest_ref, map_ref, *rest):
    outs, (held, table, seen, sem_in, sem) = rest[:skies], rest[skies:]
    load = pltpu.make_async_copy(map_ref, held.at[:, : blocks * BLK], sem_in)
    load.start()
    held[:, blocks * BLK :] = jnp.zeros((rows, BLK), F32)
    width = chans * cap

    def clear(i, carry):
        table[i] = blocks
        return carry

    lax.fori_loop(0, skies * width, clear, 0)

    def owner(c, offset):
        live = count_ref[0, c]
        for d in range(skies):
            seen[d] = 0

        def slot(j, carry):
            d = dest_ref[0, c, j]
            r = seen[d]
            seen[d] = r + 1
            table[d * width + c * cap + r] = order_ref[0, offset + j]
            return carry

        lax.fori_loop(0, live, slot, 0)
        return offset + live

    lax.fori_loop(0, chans, owner, jnp.int32(0))
    load.wait()
    for q in range(skies):
        base = (me_ref[1] ^ q) * width

        def send(i, carry, q=q, base=base):
            pltpu.make_async_copy(
                held.at[:, pl.ds(pl.multiple_of(table[base + i] * BLK, BLK), BLK)],
                outs[q].at[:, pl.ds(pl.multiple_of(i * BLK, BLK), BLK)],
                sem.at[q],
            ).start()
            return carry

        lax.fori_loop(0, width, send, 0)
    for q in range(skies):
        pltpu.make_async_copy(held.at[:, : width * BLK], outs[q], sem.at[q]).wait()


def step_kernel(step, last, sources, rows, skies, cap, *refs):
    refs = list(refs)
    take = lambda n: [refs.pop(0) for _ in range(n)]
    me_ref, count_ref, dest_ref, aux_ref = take(4)
    x_refs = take(len(sources))
    u_refs = take(step)
    sum_ref = take(1)[0] if step else None
    if last:
        amp_ref = take(1)[0]
    else:
        u_out, sum_out = take(2)
    xs, us, lower, sem_x, sem_u = take(5)
    if last:
        amp_scratch = take(1)[0]
    wide = CAP * BLK
    copies_x = []
    for i, ref in enumerate(x_refs):
        copy = pltpu.make_async_copy(ref, xs.at[i * rows : (i + 1) * rows, :wide], sem_x.at[i])
        copy.start()
        copies_x.append(copy)
    copies_u = []
    for i, ref in enumerate(u_refs):
        copy = pltpu.make_async_copy(ref, us.at[i // 2, i % 2 * STEP : (i % 2 + 1) * STEP], sem_u.at[i])
        copy.start()
        copies_u.append(copy)
    pairs = (step + 1) // 2
    if step % 2:
        us[pairs - 1, STEP:] = jnp.zeros((STEP, us.shape[2]), F32)
    for i, p in enumerate(sources):
        first = pl.multiple_of((me_ref[0] ^ p) * rows, rows)
        xs[i * rows : (i + 1) * rows, wide:] = aux_ref[pl.ds(first, rows), :]
    live = count_ref[0, me_ref[0]]
    scale = 1.0 / jnp.full((1, BLK), (live * BLK).astype(F32))
    for copy in copies_x:
        copy.wait()
    x = xs[:, :wide]
    row = lax.broadcasted_iota(jnp.int32, (STEP, BLK), 0)
    lane = lax.broadcasted_iota(jnp.int32, (STEP, BLK), 1)
    noise = xs[:, wide + TPAD : wide + TPAD + 1]
    s = dot(x, x, ((1,), (1,))) * scale + jnp.where(row == lane, noise, 0.0)
    if step:
        for copy in copies_u:
            copy.wait()

        def project(i, s):
            part = dot(x, us[i, :, :wide], ((1,), (1,))) * scale[:, :1]
            lower[i] = part
            return s - dot(part, part, ((1,), (1,)))

        s = lax.fori_loop(0, pairs, project, s)
    r = inverse_factor(s)
    if step:

        def reduce(i, carry):
            xs[...] -= dot(lower[i], us[i], ((1,), (0,)))
            return carry

        lax.fori_loop(0, pairs, reduce, 0)
    u = dot(r, xs[...], ((1,), (0,)))
    part = dot(u[:, wide : wide + TPAD], u, ((0,), (0,)))
    if step:
        part = part + sum_ref[...]
    if not last:
        u_out[...] = u
        sum_out[...] = part
        return
    row = lax.broadcasted_iota(jnp.int32, (TPAD, BLK), 0)
    lane = lax.broadcasted_iota(jnp.int32, (TPAD, BLK), 1)
    gram = jnp.where(lane < TPAD, part[:, wide:], 0.0)
    gram = gram + jnp.where((row == lane) & (row >= NT_LIVE[0]), 1.0, 0.0)
    root = panel_factor([gram[8 * g : 8 * g + 8, :] for g in range(TPAD // 8)], 0)
    root = jnp.where(lane <= row, root, 0.0)[:, :TPAD]
    amp = dot(root, dot(root, part[:, :wide], ((1,), (0,))), ((0,), (0,)))
    amp_scratch[:, :wide] = amp
    amp_scratch[:, wide:] = jnp.zeros((TPAD, BLK), F32)
    for d in range(skies):
        ranks = jnp.int32(0)
        slots = [jnp.int32(CAP)] * cap
        for j in range(CAP):
            here = (dest_ref[0, me_ref[0], j] == d) & (j < live)
            for r_ in range(cap):
                slots[r_] = jnp.where(here & (ranks == r_), j, slots[r_])
            ranks = ranks + here.astype(jnp.int32)
        for r_ in range(cap):
            at = pl.multiple_of(slots[r_] * BLK, BLK)
            amp_ref[d, :, r_ * BLK : (r_ + 1) * BLK] = amp_scratch[:, pl.ds(at, BLK)]


NT_LIVE = [30]


def split(value):
    high = value.astype(jnp.bfloat16)
    rest = value - high.astype(F32)
    middle = rest.astype(jnp.bfloat16)
    low = (rest - middle.astype(F32)).astype(jnp.bfloat16)
    return high, middle, low


def clean_kernel(chans, skies, cap, rows, me_ref, aux_ref, *rest):
    raws, amps, (out_ref, raw_scratch, sem) = rest[:skies], rest[skies : skies + chans], rest[skies + chans :]
    width = chans * cap
    copies = []
    for q in range(skies):
        copy = pltpu.make_async_copy(raws[q], raw_scratch.at[q], sem.at[q])
        copy.start()
        copies.append(copy)
    first = pl.multiple_of(me_ref[0] * rows, rows)
    high, middle, low = split(aux_ref[pl.ds(first, rows), :][:, :TPAD])
    left = jnp.concatenate([high, high, middle, middle, high, low], axis=1)
    for copy in copies:
        copy.wait()
    for p in range(chans):
        owner = me_ref[0] ^ p
        for s in range(skies):
            high, middle, low = split(amps[p][s])
            right = jnp.concatenate([high, middle, high, middle, low, high], axis=0)
            model = jnp.dot(left, right, preferred_element_type=F32)
            for r in range(cap):
                slot = owner * cap + r
                at = pl.multiple_of(slot * BLK, BLK)
                value = raw_scratch[s ^ me_ref[1], :, pl.ds(at, BLK)] - model[:, r * BLK : (r + 1) * BLK]
                out_ref[pl.ds(s * width + slot, rows, stride=skies * width), :] = value


def on_device(sky_map, templates, noise_var, block_order, patch_count, slab_dest):
    chans = lax.axis_size("chan")
    skies = lax.axis_size("sky")
    rows = sky_map.shape[0]
    nu, nt = templates.shape
    NT_LIVE[0] = nt
    blocks = block_order.shape[1]
    cap = (CAP + skies - 1) // skies
    wide = CAP * BLK
    me = jnp.stack([lax.axis_index("chan"), lax.axis_index("sky")]).astype(jnp.int32)
    aux = jnp.concatenate(
        [
            templates,
            jnp.zeros((nu, TPAD - nt), F32),
            noise_var[:, None],
            jnp.zeros((nu, BLK - TPAD - 1), F32),
        ],
        axis=1,
    )

    packed = pl.pallas_call(
        functools.partial(chan_pack_kernel, chans, blocks, rows),
        out_shape=[jax.ShapeDtypeStruct((rows, wide), F32)] * chans,
        in_specs=[SMEM, SMEM, SMEM, ANY],
        out_specs=[ANY] * chans,
        scratch_shapes=[
            pltpu.VMEM((rows, (blocks + 1) * BLK), F32),
            pltpu.SMEM((chans,), jnp.int32),
            pltpu.SemaphoreType.DMA,
            pltpu.SemaphoreType.DMA((chans,)),
        ],
        compiler_params=PARAMS,
        name="chan_pack",
    )(me, block_order, patch_count, sky_map)
    arrived = [packed[0]] + [
        lax.ppermute(packed[p], "chan", [(i, i ^ p) for i in range(chans)]) for p in range(1, chans)
    ]

    sky_packed = pl.pallas_call(
        functools.partial(sky_pack_kernel, chans, skies, cap, blocks, rows),
        out_shape=[jax.ShapeDtypeStruct((rows, chans * cap * BLK), F32)] * skies,
        in_specs=[SMEM, SMEM, SMEM, SMEM, ANY],
        out_specs=[ANY] * skies,
        scratch_shapes=[
            pltpu.VMEM((rows, (blocks + 1) * BLK), F32),
            pltpu.SMEM((skies * chans * cap,), jnp.int32),
            pltpu.SMEM((skies,), jnp.int32),
            pltpu.SemaphoreType.DMA,
            pltpu.SemaphoreType.DMA((skies,)),
        ],
        compiler_params=PARAMS,
        name="sky_pack",
    )(me, block_order, patch_count, slab_dest, sky_map)
    raws = [sky_packed[0]] + [
        lax.ppermute(sky_packed[q], "sky", [(i, i ^ q) for i in range(skies)]) for q in range(1, skies)
    ]

    per_step = STEP // rows
    steps = nu // STEP
    held = []
    total = None
    for step in range(steps):
        sources = list(range(step * per_step, (step + 1) * per_step))
        last = step == steps - 1
        if last:
            out_shape = jax.ShapeDtypeStruct((skies, TPAD, cap * BLK), F32)
            out_specs = VMEM
        else:
            out_shape = [
                jax.ShapeDtypeStruct((STEP, wide + BLK), F32),
                jax.ShapeDtypeStruct((TPAD, wide + BLK), F32),
            ]
            out_specs = [VMEM, VMEM]
        scratch = [
            pltpu.VMEM((STEP, wide + BLK), F32),
            pltpu.VMEM((max((step + 1) // 2, 1), 2 * STEP, wide + BLK), F32),
            pltpu.VMEM((max((step + 1) // 2, 1), STEP, 2 * STEP), F32),
            pltpu.SemaphoreType.DMA((per_step,)),
            pltpu.SemaphoreType.DMA((max(step, 1),)),
        ]
        if last:
            scratch.append(pltpu.VMEM((TPAD, wide + BLK), F32))
        flops = 12 * STEP * STEP * wide * (2 * step + 2)
        result = pl.pallas_call(
            functools.partial(step_kernel, step, last, sources, rows, skies, cap),
            out_shape=out_shape,
            in_specs=[SMEM, SMEM, SMEM, VMEM]
            + [ANY] * (per_step + step)
            + ([VMEM] if step else []),
            out_specs=out_specs,
            scratch_shapes=scratch,
            compiler_params=PARAMS,
            cost_estimate=pl.CostEstimate(flops=flops, bytes_accessed=(step + 2) * 600000, transcendentals=0),
            name=f"eliminate_{step}",
        )(
            me, patch_count, slab_dest, aux,
            *[arrived[p] for p in sources], *held, *([total] if step else []),
        )
        if last:
            amps = result
        else:
            held.append(result[0])
            total = result[1]

    mine = lax.all_to_all(amps, "sky", split_axis=0, concat_axis=0, tiled=True)
    spread = [mine] + [
        lax.ppermute(mine, "chan", [(i, i ^ p) for i in range(chans)]) for p in range(1, chans)
    ]
    out_rows = skies * chans * cap
    out = pl.pallas_call(
        functools.partial(clean_kernel, chans, skies, cap, rows),
        out_shape=jax.ShapeDtypeStruct((rows * out_rows, BLK), F32),
        in_specs=[SMEM, VMEM] + [ANY] * skies + [VMEM] * chans,
        out_specs=VMEM,
        scratch_shapes=[
            pltpu.VMEM((skies, rows, chans * cap * BLK), F32),
            pltpu.SemaphoreType.DMA((skies,)),
        ],
        compiler_params=PARAMS,
        name="clean",
    )(me, aux, *raws, *spread)
    return out.reshape(rows, out_rows, BLK)


def solution(mesh):
    return jax.shard_map(
        on_device,
        mesh=mesh,
        in_specs=(P("chan", "sky"), P(), P(), P("sky", None), P("sky", None), P("sky", None, None)),
        out_specs=P("chan", "sky", None),
        check_vma=False,
    )
```

```python
import functools

import jax
import jax.numpy as jnp
from jax import lax
from jax.experimental import pallas as pl
from jax.experimental.pallas import tpu as pltpu
from jax.sharding import PartitionSpec as P

BLK = 128
CAP = 8
TPAD = 32
STEP = 128
HIGHEST = lax.Precision.HIGHEST
F32 = jnp.float32
HBM = pl.BlockSpec(memory_space=pltpu.HBM)
SMEM = pl.BlockSpec(memory_space=pltpu.SMEM)
VMEM = pl.BlockSpec(memory_space=pltpu.VMEM)
PARAMS = pltpu.CompilerParams(vmem_limit_bytes=28 * 1024 * 1024)


def dot(a, b, contract):
    return lax.dot_general(
        a, b, (contract, ((), ())), precision=HIGHEST, preferred_element_type=F32
    )


def reciprocal(value):
    guess = pl.reciprocal(value, approx=True)
    guess = guess * (2.0 - value * guess)
    return guess * (2.0 - value * guess)


def panel_factor(groups, first):
    lane = lax.broadcasted_iota(jnp.int32, (8, BLK), 1)
    sub = lax.broadcasted_iota(jnp.int32, (8, BLK), 0)
    spread = lambda v, i: jnp.broadcast_to(v[i : i + 1, :], (8, BLK))
    groups = list(groups)
    count = len(groups)
    done = []
    for g in range(count):
        k = first + 8 * g
        cols = [
            [jnp.broadcast_to(groups[i][:, k + j : k + j + 1], (8, BLK)) for j in range(8)]
            for i in range(g, count)
        ]
        pivots = (lane >= k) & (lane < k + 8)
        unit = jnp.where(pivots, jnp.where(lane - k == sub, 1.0, 0.0), groups[g])
        entry = {(a, b): spread(cols[0][b], a) for a in range(8) for b in range(a + 1)}
        rows = [spread(unit, j) for j in range(8)]
        inverse = []
        lower = {}
        for j in range(8):
            inverse.append(reciprocal(entry[j, j]))
            for a in range(j + 1, 8):
                lower[a, j] = entry[a, j] * inverse[j]
            for a in range(j + 1, 8):
                for b in range(j + 1, a + 1):
                    entry[a, b] = entry[a, b] - lower[a, j] * entry[b, j]
                rows[a] = rows[a] - lower[a, j] * rows[j]
        done.append(
            jnp.concatenate([(rows[j] * lax.rsqrt(entry[j, j]))[0:1] for j in range(8)], axis=0)
        )
        if g + 1 == count:
            break
        solved = [None] * 8
        for j in reversed(range(8)):
            value = rows[j] * inverse[j]
            for m in range(j + 1, 8):
                value = value - lower[m, j] * solved[m]
            solved[j] = value
        for i in range(g + 1, count):
            terms = [cols[i - g][j] * solved[j] for j in range(8)]
            while len(terms) > 1:
                terms = [terms[q] + terms[q + 1] for q in range(0, len(terms), 2)]
            groups[i] = jnp.where(pivots, 0.0, groups[i]) - terms[0]
    return jnp.concatenate(done, axis=0)


def inverse_factor(matrix):
    wide = 32
    lane = lax.broadcasted_iota(jnp.int32, (wide, BLK), 1)
    row = lax.broadcasted_iota(jnp.int32, (wide, BLK), 0)
    groups = [matrix[8 * g : 8 * g + 8, :] for g in range(BLK // 8)]
    out = []
    for first in range(0, BLK, wide):
        last = first + wide
        panel = panel_factor(groups[first // 8 : last // 8], first)
        out.append(jnp.where(lane <= row + first, panel, 0.0))
        if last == BLK:
            break
        kept = jnp.where((lane <= row + first) | (lane >= last), panel, 0.0)
        update = dot(kept, kept, ((0,), (0,)))
        lane8 = lax.broadcasted_iota(jnp.int32, (8, BLK), 1)
        inside = (lane8 >= first) & (lane8 < last)
        for i in range(last // 8, BLK // 8):
            groups[i] = jnp.where(inside, 0.0, groups[i]) - update[8 * i : 8 * i + 8, :]
    return jnp.concatenate(out, axis=0)


def chan_pack_kernel(chans, blocks, rows, int_ref, map_ref, *rest):
    outs, (held, start, sem_in, sem) = rest[:chans], rest[chans:]
    load = pltpu.make_async_copy(map_ref, held.at[:, : blocks * BLK], sem_in)
    load.start()
    held[:, blocks * BLK :] = jnp.zeros((rows, BLK), F32)
    total = jnp.int32(0)
    for c in range(chans):
        start[c] = total
        total = total + int_ref[2 + blocks + c]
    load.wait()
    for p in list(range(1, chans)) + [0]:
        owner = int_ref[0] ^ p
        offset = start[owner]
        live = int_ref[2 + blocks + owner]
        for j in range(CAP):
            place = jnp.minimum(offset + j, blocks - 1)
            block = jnp.where(j < live, int_ref[2 + place], blocks)
            pltpu.make_async_copy(
                held.at[:, pl.ds(pl.multiple_of(block * BLK, BLK), BLK)],
                outs[p].at[:, j * BLK : (j + 1) * BLK],
                sem.at[p],
            ).start()
    for p in range(chans):
        pltpu.make_async_copy(held.at[:, : CAP * BLK], outs[p], sem.at[p]).wait()


def sky_pack_start(sizes, int_ref, map_ref, outs, held, table, seen, sem_in, sem):
    chans, skies, cap, rows, blocks, _ = sizes
    load = pltpu.make_async_copy(map_ref, held.at[:, : blocks * BLK], sem_in)
    load.start()
    held[:, blocks * BLK :] = jnp.zeros((rows, BLK), F32)
    width = chans * cap
    dests = 2 + blocks + chans

    def clear(i, carry):
        table[i] = blocks
        return carry

    lax.fori_loop(0, skies * width, clear, 0)

    def owner(c, offset):
        live = int_ref[2 + blocks + c]
        for d in range(skies):
            seen[d] = 0

        def slot(j, carry):
            d = int_ref[dests + c * CAP + j]
            r = seen[d]
            seen[d] = r + 1
            table[d * width + c * cap + r] = int_ref[2 + offset + j]
            return carry

        lax.fori_loop(0, live, slot, 0)
        return offset + live

    lax.fori_loop(0, chans, owner, jnp.int32(0))
    load.wait()
    for q in range(skies):
        base = (int_ref[1] ^ q) * width

        def send(i, carry, q=q, base=base):
            pltpu.make_async_copy(
                held.at[:, pl.ds(pl.multiple_of(table[base + i] * BLK, BLK), BLK)],
                outs[q].at[:, pl.ds(pl.multiple_of(i * BLK, BLK), BLK)],
                sem.at[q],
            ).start()
            return carry

        lax.fori_loop(0, width, send, 0)
    return [pltpu.make_async_copy(held.at[:, : width * BLK], outs[q], sem.at[q]) for q in range(skies)]


def eliminate_kernel(before, parts, last, merge, sources, sizes, *refs):
    chans, skies, cap, rows, blocks, nt = sizes
    refs = list(refs)
    take = lambda n: [refs.pop(0) for _ in range(n)]
    (int_ref,) = take(1)
    if before:
        (aux_ref,) = take(1)
    else:
        template_ref, noise_ref, map_ref = take(3)
    x_refs = take(len(sources))
    u_refs = take(before)
    sum_ref = take(1)[0] if before else None
    if last:
        (amp_ref,) = take(1)
    else:
        u_out, sum_out = take(2)
    if not before:
        (aux_ref,) = take(1)
        sky_out = take(skies)
    (xs,) = take(1)
    if last:
        (amp_scratch,) = take(1)
    wide = CAP * BLK
    size = parts * STEP
    packs = [] if before else sky_pack_start(sizes, int_ref, map_ref, sky_out, *refs)
    if not before:
        for at in range(0, aux_ref.shape[0], BLK):
            tall = jnp.concatenate(
                [
                    template_ref[:, at : at + BLK],
                    jnp.zeros((TPAD - nt, BLK), F32),
                    jnp.broadcast_to(noise_ref[:, at : at + BLK], (BLK - TPAD, BLK)),
                ],
                axis=0,
            )
            aux_ref[at : at + BLK, :] = tall.T
    for i, p in enumerate(sources):
        first = pl.multiple_of((int_ref[0] ^ p) * rows, rows)
        xs[i * rows : (i + 1) * rows, :wide] = x_refs[i][...]
        xs[i * rows : (i + 1) * rows, wide:] = aux_ref[pl.ds(first, rows), :]
    live = int_ref[2 + blocks + int_ref[0]]
    scale = 1.0 / jnp.full((1, BLK), (live * BLK).astype(F32))[:, :1]
    x = xs[:, :wide]
    row = lax.broadcasted_iota(jnp.int32, (size, size), 0)
    lane = lax.broadcasted_iota(jnp.int32, (size, size), 1)
    noise = xs[:, wide + TPAD : wide + TPAD + 1]
    s = dot(x, x, ((1,), (1,))) * scale + jnp.where(row == lane, noise, 0.0)
    lower = []
    for ref in u_refs:
        part = dot(x, ref[:, :wide], ((1,), (1,))) * scale
        s = s - dot(part, part, ((1,), (1,)))
        lower.append(part)
    value = xs[...]
    for part, ref in zip(lower, u_refs):
        value = value - dot(part, ref[...], ((1,), (0,)))
    r = inverse_factor(s[:STEP, :STEP])
    u = dot(r, value[:STEP], ((1,), (0,)))
    if parts == 2:
        side = dot(s[STEP:, :STEP], r, ((1,), (1,)))
        r2 = inverse_factor(s[STEP:, STEP:] - dot(side, side, ((1,), (1,))))
        u2 = dot(r2, value[STEP:] - dot(side, u, ((1,), (0,))), ((1,), (0,)))
        u = jnp.concatenate([u, u2], axis=0)
    part = dot(u[:, wide : wide + TPAD], u, ((0,), (0,)))
    if before:
        part = part + sum_ref[...]
    if not last:
        if merge:
            u_out[: STEP] = u_refs[0][...]
            u_out[STEP:] = u
        else:
            u_out[...] = u
        sum_out[...] = part
        for pack in packs:
            pack.wait()
        return
    row = lax.broadcasted_iota(jnp.int32, (TPAD, BLK), 0)
    lane = lax.broadcasted_iota(jnp.int32, (TPAD, BLK), 1)
    gram = jnp.where(lane < TPAD, part[:, wide:], 0.0)
    gram = gram + jnp.where((row == lane) & (row >= nt), 1.0, 0.0)
    root = panel_factor([gram[8 * g : 8 * g + 8, :] for g in range(TPAD // 8)], 0)
    root = jnp.where(lane <= row, root, 0.0)[:, :TPAD]
    amp = dot(root, dot(root, part[:, :wide], ((1,), (0,))), ((0,), (0,)))
    amp_scratch[:, :wide] = amp
    amp_scratch[:, wide:] = jnp.zeros((TPAD, BLK), F32)
    dests = 2 + blocks + chans + int_ref[0] * CAP
    for d in range(skies):
        ranks = jnp.int32(0)
        slots = [jnp.int32(CAP)] * cap
        for j in range(CAP):
            here = (int_ref[dests + j] == d) & (j < live)
            for rank in range(cap):
                slots[rank] = jnp.where(here & (ranks == rank), j, slots[rank])
            ranks = ranks + here.astype(jnp.int32)
        for rank in range(cap):
            at = pl.multiple_of(slots[rank] * BLK, BLK)
            amp_ref[d, :, rank * BLK : (rank + 1) * BLK] = amp_scratch[:, pl.ds(at, BLK)]


def split(value):
    high = value.astype(jnp.bfloat16)
    rest = value - high.astype(F32)
    middle = rest.astype(jnp.bfloat16)
    low = (rest - middle.astype(F32)).astype(jnp.bfloat16)
    return high, middle, low


def clean_kernel(chans, skies, cap, rows, int_ref, aux_ref, *rest):
    raws, amps, (out_ref, raw_scratch, sem) = rest[:skies], rest[skies : skies + chans], rest[skies + chans :]
    width = chans * cap
    copies = []
    for q in range(skies):
        copy = pltpu.make_async_copy(raws[q], raw_scratch.at[q], sem.at[q])
        copy.start()
        copies.append(copy)
    first = pl.multiple_of(int_ref[0] * rows, rows)
    high, middle, low = split(aux_ref[pl.ds(first, rows), :][:, :TPAD])
    left = jnp.concatenate([high, high, middle, middle, high, low], axis=1)
    for copy in copies:
        copy.wait()
    for p in range(chans):
        owner = int_ref[0] ^ p
        for s in range(skies):
            high, middle, low = split(amps[p][s])
            right = jnp.concatenate([high, middle, high, middle, low, high], axis=0)
            model = jnp.dot(left, right, preferred_element_type=F32)
            for r in range(cap):
                slot = owner * cap + r
                at = pl.multiple_of(slot * BLK, BLK)
                value = raw_scratch[s ^ int_ref[1], :, pl.ds(at, BLK)] - model[:, r * BLK : (r + 1) * BLK]
                out_ref[pl.ds(s * width + slot, rows, stride=skies * width), :] = value


def swap(value, axis, bits):
    size = lax.axis_size(axis)
    return lax.ppermute(value, axis, [(i, i ^ bits) for i in range(size)])


def share(value, chans):
    known = {0: value}
    known[1] = swap(value, "chan", 1)
    bit = chans // 2
    while bit > 1:
        for p in sorted(k for k in known if k % 2 == 0):
            known[p ^ bit] = swap(known[p], "chan", bit)
        bit //= 2
    for p in sorted(k for k in known if k % 2 == 0 and k):
        known[p ^ 1] = swap(known[p], "chan", 1)
    return [known[p] for p in range(chans)]


def on_device(sky_map, templates, noise_var, block_order, patch_count, slab_dest):
    chans = lax.axis_size("chan")
    skies = lax.axis_size("sky")
    rows = sky_map.shape[0]
    nu, nt = templates.shape
    blocks = block_order.shape[1]
    cap = (CAP + skies - 1) // skies
    wide = CAP * BLK
    sizes = (chans, skies, cap, rows, blocks, nt)
    place = jnp.stack([lax.axis_index("chan"), lax.axis_index("sky")]).astype(jnp.int32)
    ints = jnp.concatenate([place, block_order[0], patch_count[0], slab_dest[0].reshape(-1)])

    packed = pl.pallas_call(
        functools.partial(chan_pack_kernel, chans, blocks, rows),
        out_shape=[jax.ShapeDtypeStruct((rows, wide), F32)] * chans,
        in_specs=[SMEM, HBM],
        out_specs=[HBM] * chans,
        scratch_shapes=[
            pltpu.VMEM((rows, (blocks + 1) * BLK), F32),
            pltpu.SMEM((chans,), jnp.int32),
            pltpu.SemaphoreType.DMA,
            pltpu.SemaphoreType.DMA((chans,)),
        ],
        compiler_params=PARAMS,
        name="chan_pack",
    )(ints, sky_map)
    arrived = {0: packed[0]}

    def fetch(block, after):
        for p in range(block * per_step, (block + 1) * per_step):
            if p:
                parcel = packed[p] if after is None else lax.optimization_barrier((packed[p], after))[0]
                arrived[p] = swap(parcel, "chan", p)

    per_step = STEP // rows
    steps = nu // STEP
    groups = [[0], [1]] + [[i, i + 1] for i in range(2, steps, 2)]
    starts = {-1: list(range(steps))}
    sky_starts = {1: list(range(1, skies))}
    for block in starts[-1]:
        fetch(block, None)
    held = []
    before = []
    for turn, group in enumerate(groups):
        parts = len(group)
        done = sum(before)
        sources = [p for block in group for p in range(block * per_step, (block + 1) * per_step)]
        last = done + parts == steps
        if last:
            for q in range(1, skies):
                total, raws[q] = lax.optimization_barrier((total, raws[q]))
        size = parts * STEP
        merge = turn == 1
        if last:
            out_shape = [jax.ShapeDtypeStruct((skies, TPAD, cap * BLK), F32)]
        else:
            out_shape = [
                jax.ShapeDtypeStruct((size + merge * STEP, wide + BLK), F32),
                jax.ShapeDtypeStruct((TPAD, wide + BLK), F32),
            ]
            if not before:
                out_shape.append(jax.ShapeDtypeStruct((nu, BLK), F32))
                out_shape += [jax.ShapeDtypeStruct((rows, chans * cap * BLK), F32)] * skies
        scratch = [
            pltpu.VMEM((size, wide + BLK), F32),
        ]
        if last:
            scratch.append(pltpu.VMEM((TPAD, wide + BLK), F32))
        if not before:
            scratch += [
                pltpu.VMEM((rows, (blocks + 1) * BLK), F32),
                pltpu.SMEM((skies * chans * cap,), jnp.int32),
                pltpu.SMEM((skies,), jnp.int32),
                pltpu.SemaphoreType.DMA,
                pltpu.SemaphoreType.DMA((skies,)),
            ]
        result = pl.pallas_call(
            functools.partial(eliminate_kernel, len(held), parts, last, merge, sources, sizes),
            out_shape=out_shape,
            in_specs=[SMEM]
            + ([VMEM] if before else [VMEM, VMEM, HBM])
            + [VMEM] * (len(sources) + len(held) + bool(before)),
            out_specs=[VMEM] * min(len(out_shape), 3) + [HBM] * max(len(out_shape) - 3, 0),
            scratch_shapes=scratch,
            compiler_params=PARAMS,
            cost_estimate=pl.CostEstimate(
                flops=12 * size * STEP * wide * (2 * done + 2), bytes_accessed=(done + 2) * 600000, transcendentals=0
            ),
            name=f"eliminate_{done}",
        )(
            ints,
            *([aux] if before else [templates.T, noise_var.reshape(1, nu), sky_map]),
            *[arrived[p] for p in sources],
            *held,
            *([total] if before else []),
        )
        if last:
            amps = result[0]
            break
        if not before:
            aux = result[2]
            sky_packed = result[3:]
        held = [result[0]] if merge else held + [result[0]]
        total = result[1]
        before.append(parts)
        for block in starts.get(turn, []):
            fetch(block, total)
        if turn == 0:
            raws = {0: result[3]}
        for q in sky_starts.get(turn, []):
            if q < skies:
                raws[q] = swap(lax.optimization_barrier((sky_packed[q], total))[0], "sky", q)

    mine = lax.all_to_all(amps, "sky", split_axis=0, concat_axis=0, tiled=True)
    shared = share(mine, chans)
    out_rows = skies * chans * cap
    out = pl.pallas_call(
        functools.partial(clean_kernel, chans, skies, cap, rows),
        out_shape=jax.ShapeDtypeStruct((rows * out_rows, BLK), F32),
        in_specs=[SMEM, VMEM] + [HBM] * skies + [VMEM] * chans,
        out_specs=VMEM,
        scratch_shapes=[
            pltpu.VMEM((skies, rows, chans * cap * BLK), F32),
            pltpu.SemaphoreType.DMA((skies,)),
        ],
        compiler_params=PARAMS,
        name="clean",
    )(ints, aux, *[raws[q] for q in range(skies)], *shared)
    return out.reshape(rows, out_rows, BLK)


def solution(mesh):
    return jax.shard_map(
        on_device,
        mesh=mesh,
        in_specs=(P("chan", "sky"), P(), P(), P("sky", None), P("sky", None), P("sky", None, None)),
        out_specs=P("chan", "sky", None),
        check_vma=False,
    )
```

```python
import functools

import jax
import jax.numpy as jnp
from jax import lax
from jax.experimental import pallas as pl
from jax.experimental.pallas import tpu as pltpu
from jax.sharding import PartitionSpec as P

BLK = 128
CAP = 8
TPAD = 32
STEP = 128
HIGHEST = lax.Precision.HIGHEST
F32 = jnp.float32
HBM = pl.BlockSpec(memory_space=pltpu.HBM)
SMEM = pl.BlockSpec(memory_space=pltpu.SMEM)
VMEM = pl.BlockSpec(memory_space=pltpu.VMEM)
PARAMS = pltpu.CompilerParams(vmem_limit_bytes=28 * 1024 * 1024)


def dot(a, b, contract):
    return lax.dot_general(
        a, b, (contract, ((), ())), precision=HIGHEST, preferred_element_type=F32
    )


def reciprocal(value):
    guess = pl.reciprocal(value, approx=True)
    return guess * (2.0 - value * guess)


def split(value):
    high = value.astype(jnp.bfloat16)
    rest = value - high.astype(F32)
    middle = rest.astype(jnp.bfloat16)
    low = (rest - middle.astype(F32)).astype(jnp.bfloat16)
    return high, middle, low


def panel_factor(groups, first):
    lane = lax.broadcasted_iota(jnp.int32, (8, BLK), 1)
    sub = lax.broadcasted_iota(jnp.int32, (8, BLK), 0)
    spread = lambda v, i: jnp.broadcast_to(v[i : i + 1, :], (8, BLK))
    groups = list(groups)
    count = len(groups)
    done = []
    for g in range(count):
        k = first + 8 * g
        cols = [
            [jnp.broadcast_to(groups[i][:, k + j : k + j + 1], (8, BLK)) for j in range(8)]
            for i in range(g, count)
        ]
        pivots = (lane >= k) & (lane < k + 8)
        unit = jnp.where(pivots, jnp.where(lane - k == sub, 1.0, 0.0), groups[g])
        entry = {(a, b): spread(cols[0][b], a) for a in range(8) for b in range(a + 1)}
        rows = [spread(unit, j) for j in range(8)]
        inverse = []
        lower = {}
        for j in range(8):
            inverse.append(reciprocal(entry[j, j]))
            for a in range(j + 1, 8):
                lower[a, j] = entry[a, j] * inverse[j]
            for a in range(j + 1, 8):
                for b in range(j + 1, a + 1):
                    entry[a, b] = entry[a, b] - lower[a, j] * entry[b, j]
                rows[a] = rows[a] - lower[a, j] * rows[j]
        done.append(
            jnp.concatenate([(rows[j] * lax.rsqrt(entry[j, j]))[0:1] for j in range(8)], axis=0)
        )
        if g + 1 == count:
            break
        solved = [None] * 8
        for j in reversed(range(8)):
            value = rows[j] * inverse[j]
            for m in range(j + 1, 8):
                value = value - lower[m, j] * solved[m]
            solved[j] = value
        for i in range(g + 1, count):
            terms = [cols[i - g][j] * solved[j] for j in range(8)]
            while len(terms) > 1:
                terms = [terms[q] + terms[q + 1] for q in range(0, len(terms), 2)]
            groups[i] = jnp.where(pivots, 0.0, groups[i]) - terms[0]
    return jnp.concatenate(done, axis=0)


def inverse_factor(matrix):
    wide = 32
    lane = lax.broadcasted_iota(jnp.int32, (wide, BLK), 1)
    row = lax.broadcasted_iota(jnp.int32, (wide, BLK), 0)
    groups = [matrix[8 * g : 8 * g + 8, :] for g in range(BLK // 8)]
    out = []
    for first in range(0, BLK, wide):
        last = first + wide
        panel = panel_factor(groups[first // 8 : last // 8], first)
        out.append(jnp.where(lane <= row + first, panel, 0.0))
        if last == BLK:
            break
        kept = jnp.where((lane <= row + first) | (lane >= last), panel, 0.0)
        high, middle, low = split(kept)
        update = lax.dot_general(
            jnp.concatenate([high, high, middle, middle, high, low], axis=0),
            jnp.concatenate([high, middle, high, middle, low, high], axis=0),
            (((0,), (0,)), ((), ())),
            preferred_element_type=F32,
        )
        lane8 = lax.broadcasted_iota(jnp.int32, (8, BLK), 1)
        inside = (lane8 >= first) & (lane8 < last)
        for i in range(last // 8, BLK // 8):
            groups[i] = jnp.where(inside, 0.0, groups[i]) - update[8 * i : 8 * i + 8, :]
    return jnp.concatenate(out, axis=0)


def chan_pack_kernel(chans, blocks, rows, int_ref, map_ref, *rest):
    outs, (held, start, sem_in, sem) = rest[:chans], rest[chans:]
    load = pltpu.make_async_copy(map_ref, held.at[:, : blocks * BLK], sem_in)
    load.start()
    held[:, blocks * BLK :] = jnp.zeros((rows, BLK), F32)
    total = jnp.int32(0)
    for c in range(chans):
        start[c] = total
        total = total + int_ref[2 + blocks + c]
    load.wait()
    for p in list(range(1, chans)) + [0]:
        owner = int_ref[0] ^ p
        offset = start[owner]
        live = int_ref[2 + blocks + owner]
        for j in range(CAP):
            place = jnp.minimum(offset + j, blocks - 1)
            block = jnp.where(j < live, int_ref[2 + place], blocks)
            pltpu.make_async_copy(
                held.at[:, pl.ds(pl.multiple_of(block * BLK, BLK), BLK)],
                outs[p].at[:, j * BLK : (j + 1) * BLK],
                sem.at[p],
            ).start()
    for p in range(chans):
        pltpu.make_async_copy(held.at[:, : CAP * BLK], outs[p], sem.at[p]).wait()


def sky_pack_start(sizes, int_ref, map_ref, outs, held, table, seen, sem_in, sem):
    chans, skies, cap, rows, blocks, _ = sizes
    load = pltpu.make_async_copy(map_ref, held.at[:, : blocks * BLK], sem_in)
    load.start()
    held[:, blocks * BLK :] = jnp.zeros((rows, BLK), F32)
    width = chans * cap
    dests = 2 + blocks + chans

    def clear(i, carry):
        table[i] = blocks
        return carry

    lax.fori_loop(0, skies * width, clear, 0)

    def owner(c, offset):
        live = int_ref[2 + blocks + c]
        for d in range(skies):
            seen[d] = 0

        def slot(j, carry):
            d = int_ref[dests + c * CAP + j]
            r = seen[d]
            seen[d] = r + 1
            table[d * width + c * cap + r] = int_ref[2 + offset + j]
            return carry

        lax.fori_loop(0, live, slot, 0)
        return offset + live

    lax.fori_loop(0, chans, owner, jnp.int32(0))
    load.wait()
    for q in range(skies):
        base = (int_ref[1] ^ q) * width

        def send(i, carry, q=q, base=base):
            pltpu.make_async_copy(
                held.at[:, pl.ds(pl.multiple_of(table[base + i] * BLK, BLK), BLK)],
                outs[q].at[:, pl.ds(pl.multiple_of(i * BLK, BLK), BLK)],
                sem.at[q],
            ).start()
            return carry

        lax.fori_loop(0, width, send, 0)
    return [pltpu.make_async_copy(held.at[:, : width * BLK], outs[q], sem.at[q]) for q in range(skies)]


def eliminate_kernel(before, parts, last, merge, sources, sizes, *refs):
    chans, skies, cap, rows, blocks, nt = sizes
    refs = list(refs)
    take = lambda n: [refs.pop(0) for _ in range(n)]
    (int_ref,) = take(1)
    if before:
        (aux_ref,) = take(1)
    else:
        template_ref, noise_ref, map_ref = take(3)
    x_refs = take(len(sources))
    u_refs = take(before)
    sum_ref = take(1)[0] if before else None
    if last:
        (amp_ref,) = take(1)
    else:
        u_out, sum_out = take(2)
    if not before:
        (aux_ref,) = take(1)
        sky_out = take(skies)
    (xs,) = take(1)
    if last:
        (amp_scratch,) = take(1)
    wide = CAP * BLK
    size = parts * STEP
    packs = [] if before else sky_pack_start(sizes, int_ref, map_ref, sky_out, *refs)
    if not before:
        for at in range(0, aux_ref.shape[0], BLK):
            tall = jnp.concatenate(
                [
                    template_ref[:, at : at + BLK],
                    jnp.zeros((TPAD - nt, BLK), F32),
                    jnp.broadcast_to(noise_ref[:, at : at + BLK], (BLK - TPAD, BLK)),
                ],
                axis=0,
            )
            aux_ref[at : at + BLK, :] = tall.T
    for i, p in enumerate(sources):
        first = pl.multiple_of((int_ref[0] ^ p) * rows, rows)
        xs[i * rows : (i + 1) * rows, :wide] = x_refs[i][...]
        xs[i * rows : (i + 1) * rows, wide:] = aux_ref[pl.ds(first, rows), :]
    live = int_ref[2 + blocks + int_ref[0]]
    scale = 1.0 / jnp.full((1, BLK), (live * BLK).astype(F32))[:, :1]
    x = xs[:, :wide]
    row = lax.broadcasted_iota(jnp.int32, (size, size), 0)
    lane = lax.broadcasted_iota(jnp.int32, (size, size), 1)
    noise = xs[:, wide + TPAD : wide + TPAD + 1]
    s = dot(x, x, ((1,), (1,))) * scale + jnp.where(row == lane, noise, 0.0)
    lower = []
    for ref in u_refs:
        part = dot(x, ref[:, :wide], ((1,), (1,))) * scale
        s = s - dot(part, part, ((1,), (1,)))
        lower.append(part)
    value = xs[...]
    for part, ref in zip(lower, u_refs):
        value = value - dot(part, ref[...], ((1,), (0,)))
    r = inverse_factor(s[:STEP, :STEP])
    u = dot(r, value[:STEP], ((1,), (0,)))
    if parts == 2:
        side = dot(s[STEP:, :STEP], r, ((1,), (1,)))
        r2 = inverse_factor(s[STEP:, STEP:] - dot(side, side, ((1,), (1,))))
        u2 = dot(r2, value[STEP:] - dot(side, u, ((1,), (0,))), ((1,), (0,)))
        u = jnp.concatenate([u, u2], axis=0)
    part = dot(u[:, wide : wide + TPAD], u, ((0,), (0,)))
    if before:
        part = part + sum_ref[...]
    if not last:
        if merge:
            u_out[: STEP] = u_refs[0][...]
            u_out[STEP:] = u
        else:
            u_out[...] = u
        sum_out[...] = part
        for pack in packs:
            pack.wait()
        return
    row = lax.broadcasted_iota(jnp.int32, (TPAD, BLK), 0)
    lane = lax.broadcasted_iota(jnp.int32, (TPAD, BLK), 1)
    gram = jnp.where(lane < TPAD, part[:, wide:], 0.0)
    gram = gram + jnp.where((row == lane) & (row >= nt), 1.0, 0.0)
    root = panel_factor([gram[8 * g : 8 * g + 8, :] for g in range(TPAD // 8)], 0)
    root = jnp.where(lane <= row, root, 0.0)[:, :TPAD]
    amp = dot(root, dot(root, part[:, :wide], ((1,), (0,))), ((0,), (0,)))
    amp_scratch[:, :wide] = amp
    amp_scratch[:, wide:] = jnp.zeros((TPAD, BLK), F32)
    dests = 2 + blocks + chans + int_ref[0] * CAP
    for d in range(skies):
        ranks = jnp.int32(0)
        slots = [jnp.int32(CAP)] * cap
        for j in range(CAP):
            here = (int_ref[dests + j] == d) & (j < live)
            for rank in range(cap):
                slots[rank] = jnp.where(here & (ranks == rank), j, slots[rank])
            ranks = ranks + here.astype(jnp.int32)
        for rank in range(cap):
            at = pl.multiple_of(slots[rank] * BLK, BLK)
            amp_ref[d, :, rank * BLK : (rank + 1) * BLK] = amp_scratch[:, pl.ds(at, BLK)]


def clean_kernel(chans, skies, cap, rows, int_ref, aux_ref, *rest):
    raws, amps = rest[:skies], rest[skies : skies + chans]
    out_ref, raw_scratch, out_scratch, sem, out_sem = rest[skies + chans :]
    width = chans * cap
    copies = []
    for q in range(skies):
        copy = pltpu.make_async_copy(raws[q], raw_scratch.at[q], sem.at[q])
        copy.start()
        copies.append(copy)
    first = pl.multiple_of(int_ref[0] * rows, rows)
    high, middle, low = split(aux_ref[pl.ds(first, rows), :][:, :TPAD])
    left = jnp.concatenate([high, high, middle, middle, high, low], axis=1)
    stores = []
    for q in range(skies):
        s = int_ref[1] ^ q
        copies[q].wait()
        for p in range(chans):
            owner = int_ref[0] ^ p
            high, middle, low = split(amps[p][s])
            right = jnp.concatenate([high, middle, high, middle, low, high], axis=0)
            model = jnp.dot(left, right, preferred_element_type=F32)
            for r in range(cap):
                slot = owner * cap + r
                at = pl.multiple_of(slot * BLK, BLK)
                value = raw_scratch[q, :, pl.ds(at, BLK)] - model[:, r * BLK : (r + 1) * BLK]
                out_scratch[q, pl.ds(slot, rows, stride=width), :] = value
        store = pltpu.make_async_copy(
            out_scratch.at[q].reshape(rows, width, BLK),
            out_ref.at[:, pl.ds(pl.multiple_of(s * width, width), width), :],
            out_sem.at[q],
        )
        store.start()
        stores.append(store)
    for store in stores:
        store.wait()


def swap(value, axis, bits):
    size = lax.axis_size(axis)
    return lax.ppermute(value, axis, [(i, i ^ bits) for i in range(size)])


def share(value, chans):
    known = {0: value}
    known[1] = swap(value, "chan", 1)
    bit = chans // 2
    while bit > 1:
        for p in sorted(k for k in known if k % 2 == 0):
            known[p ^ bit] = swap(known[p], "chan", bit)
        bit //= 2
    for p in sorted(k for k in known if k % 2 == 0 and k):
        known[p ^ 1] = swap(known[p], "chan", 1)
    return [known[p] for p in range(chans)]


def on_device(sky_map, templates, noise_var, block_order, patch_count, slab_dest):
    chans = lax.axis_size("chan")
    skies = lax.axis_size("sky")
    rows = sky_map.shape[0]
    nu, nt = templates.shape
    blocks = block_order.shape[1]
    cap = (CAP + skies - 1) // skies
    wide = CAP * BLK
    sizes = (chans, skies, cap, rows, blocks, nt)
    place = jnp.stack([lax.axis_index("chan"), lax.axis_index("sky")]).astype(jnp.int32)
    ints = jnp.concatenate([place, block_order[0], patch_count[0], slab_dest[0].reshape(-1)])

    packed = pl.pallas_call(
        functools.partial(chan_pack_kernel, chans, blocks, rows),
        out_shape=[jax.ShapeDtypeStruct((rows, wide), F32)] * chans,
        in_specs=[SMEM, HBM],
        out_specs=[HBM] * chans,
        scratch_shapes=[
            pltpu.VMEM((rows, (blocks + 1) * BLK), F32),
            pltpu.SMEM((chans,), jnp.int32),
            pltpu.SemaphoreType.DMA,
            pltpu.SemaphoreType.DMA((chans,)),
        ],
        compiler_params=PARAMS,
        name="chan_pack",
    )(ints, sky_map)
    arrived = {0: packed[0]}

    def fetch(block, after):
        for p in range(block * per_step, (block + 1) * per_step):
            if p:
                parcel = packed[p] if after is None else lax.optimization_barrier((packed[p], after))[0]
                arrived[p] = swap(parcel, "chan", p)

    per_step = STEP // rows
    steps = nu // STEP
    groups = [[0], [1]] + [[i, i + 1] for i in range(2, steps, 2)]
    starts = {-1: list(range(steps))}
    sky_starts = {1: list(range(1, skies))}
    for block in starts[-1]:
        fetch(block, None)
    held = []
    before = []
    for turn, group in enumerate(groups):
        parts = len(group)
        done = sum(before)
        sources = [p for block in group for p in range(block * per_step, (block + 1) * per_step)]
        last = done + parts == steps
        if last:
            for q in range(1, skies):
                total, raws[q] = lax.optimization_barrier((total, raws[q]))
        size = parts * STEP
        merge = turn == 1
        if last:
            out_shape = [jax.ShapeDtypeStruct((skies, TPAD, cap * BLK), F32)]
        else:
            out_shape = [
                jax.ShapeDtypeStruct((size + merge * STEP, wide + BLK), F32),
                jax.ShapeDtypeStruct((TPAD, wide + BLK), F32),
            ]
            if not before:
                out_shape.append(jax.ShapeDtypeStruct((nu, BLK), F32))
                out_shape += [jax.ShapeDtypeStruct((rows, chans * cap * BLK), F32)] * skies
        scratch = [
            pltpu.VMEM((size, wide + BLK), F32),
        ]
        if last:
            scratch.append(pltpu.VMEM((TPAD, wide + BLK), F32))
        if not before:
            scratch += [
                pltpu.VMEM((rows, (blocks + 1) * BLK), F32),
                pltpu.SMEM((skies * chans * cap,), jnp.int32),
                pltpu.SMEM((skies,), jnp.int32),
                pltpu.SemaphoreType.DMA,
                pltpu.SemaphoreType.DMA((skies,)),
            ]
        result = pl.pallas_call(
            functools.partial(eliminate_kernel, len(held), parts, last, merge, sources, sizes),
            out_shape=out_shape,
            in_specs=[SMEM]
            + ([VMEM] if before else [VMEM, VMEM, HBM])
            + [VMEM] * (len(sources) + len(held) + bool(before)),
            out_specs=[VMEM] * min(len(out_shape), 3) + [HBM] * max(len(out_shape) - 3, 0),
            scratch_shapes=scratch,
            compiler_params=PARAMS,
            cost_estimate=pl.CostEstimate(
                flops=12 * size * STEP * wide * (2 * done + 2), bytes_accessed=(done + 2) * 600000, transcendentals=0
            ),
            name=f"eliminate_{done}",
        )(
            ints,
            *([aux] if before else [templates.T, noise_var.reshape(1, nu), sky_map]),
            *[arrived[p] for p in sources],
            *held,
            *([total] if before else []),
        )
        if last:
            amps = result[0]
            break
        if not before:
            aux = result[2]
            sky_packed = result[3:]
        held = [result[0]] if merge else held + [result[0]]
        total = result[1]
        before.append(parts)
        for block in starts.get(turn, []):
            fetch(block, total)
        if turn == 0:
            raws = {0: result[3]}
        for q in sky_starts.get(turn, []):
            if q < skies:
                raws[q] = swap(lax.optimization_barrier((sky_packed[q], total))[0], "sky", q)

    mine = lax.all_to_all(amps, "sky", split_axis=0, concat_axis=0, tiled=True)
    shared = share(mine, chans)
    out_rows = skies * chans * cap
    return pl.pallas_call(
        functools.partial(clean_kernel, chans, skies, cap, rows),
        out_shape=jax.ShapeDtypeStruct((rows, out_rows, BLK), F32),
        in_specs=[SMEM, VMEM] + [HBM] * skies + [VMEM] * chans,
        out_specs=HBM,
        scratch_shapes=[
            pltpu.VMEM((skies, rows, chans * cap * BLK), F32),
            pltpu.VMEM((skies, rows * chans * cap, BLK), F32),
            pltpu.SemaphoreType.DMA((skies,)),
            pltpu.SemaphoreType.DMA((skies,)),
        ],
        compiler_params=PARAMS,
        name="clean",
    )(ints, aux, *[raws[q] for q in range(skies)], *shared)


def solution(mesh):
    return jax.shard_map(
        on_device,
        mesh=mesh,
        in_specs=(P("chan", "sky"), P(), P(), P("sky", None), P("sky", None), P("sky", None, None)),
        out_specs=P("chan", "sky", None),
        check_vma=False,
    )
```

```python
import functools

import jax
import jax.numpy as jnp
from jax import lax
from jax.experimental import pallas as pl
from jax.experimental.pallas import tpu as pltpu
from jax.sharding import PartitionSpec as P

BLK = 128
CAP = 8
TPAD = 32
STEP = 128
HIGHEST = lax.Precision.HIGHEST
F32 = jnp.float32
HBM = pl.BlockSpec(memory_space=pltpu.HBM)
SMEM = pl.BlockSpec(memory_space=pltpu.SMEM)
VMEM = pl.BlockSpec(memory_space=pltpu.VMEM)
PARAMS = pltpu.CompilerParams(vmem_limit_bytes=28 * 1024 * 1024)


def dot(a, b, contract):
    return lax.dot_general(
        a, b, (contract, ((), ())), precision=HIGHEST, preferred_element_type=F32
    )


def reciprocal(value):
    guess = pl.reciprocal(value, approx=True)
    return guess * (2.0 - value * guess)


def split(value):
    high = value.astype(jnp.bfloat16)
    rest = value - high.astype(F32)
    middle = rest.astype(jnp.bfloat16)
    low = (rest - middle.astype(F32)).astype(jnp.bfloat16)
    return high, middle, low


def panel_factor(groups, first):
    lane = lax.broadcasted_iota(jnp.int32, (8, BLK), 1)
    sub = lax.broadcasted_iota(jnp.int32, (8, BLK), 0)
    spread = lambda v, i: jnp.broadcast_to(v[i : i + 1, :], (8, BLK))
    groups = list(groups)
    count = len(groups)
    done = []
    for g in range(count):
        k = first + 8 * g
        cols = [
            [jnp.broadcast_to(groups[i][:, k + j : k + j + 1], (8, BLK)) for j in range(8)]
            for i in range(g, count)
        ]
        pivots = (lane >= k) & (lane < k + 8)
        unit = jnp.where(pivots, jnp.where(lane - k == sub, 1.0, 0.0), groups[g])
        entry = {(a, b): spread(cols[0][b], a) for a in range(8) for b in range(a + 1)}
        rows = [spread(unit, j) for j in range(8)]
        inverse = []
        lower = {}
        for j in range(8):
            inverse.append(reciprocal(entry[j, j]))
            for a in range(j + 1, 8):
                lower[a, j] = entry[a, j] * inverse[j]
            for a in range(j + 1, 8):
                for b in range(j + 1, a + 1):
                    entry[a, b] = entry[a, b] - lower[a, j] * entry[b, j]
                rows[a] = rows[a] - lower[a, j] * rows[j]
        done.append(
            jnp.concatenate([(rows[j] * lax.rsqrt(entry[j, j]))[0:1] for j in range(8)], axis=0)
        )
        if g + 1 == count:
            break
        solved = [None] * 8
        for j in reversed(range(8)):
            value = rows[j] * inverse[j]
            for m in range(j + 1, 8):
                value = value - lower[m, j] * solved[m]
            solved[j] = value
        for i in range(g + 1, count):
            terms = [cols[i - g][j] * solved[j] for j in range(8)]
            while len(terms) > 1:
                terms = [terms[q] + terms[q + 1] for q in range(0, len(terms), 2)]
            groups[i] = jnp.where(pivots, 0.0, groups[i]) - terms[0]
    return jnp.concatenate(done, axis=0)


def inverse_factor(matrix):
    wide = 32
    lane = lax.broadcasted_iota(jnp.int32, (wide, BLK), 1)
    row = lax.broadcasted_iota(jnp.int32, (wide, BLK), 0)
    groups = [matrix[8 * g : 8 * g + 8, :] for g in range(BLK // 8)]
    out = []
    for first in range(0, BLK, wide):
        last = first + wide
        panel = panel_factor(groups[first // 8 : last // 8], first)
        out.append(jnp.where(lane <= row + first, panel, 0.0))
        if last == BLK:
            break
        kept = jnp.where((lane <= row + first) | (lane >= last), panel, 0.0)
        high, middle, low = split(kept)
        update = lax.dot_general(
            jnp.concatenate([high, high, middle, middle, high, low], axis=0),
            jnp.concatenate([high, middle, high, middle, low, high], axis=0),
            (((0,), (0,)), ((), ())),
            preferred_element_type=F32,
        )
        lane8 = lax.broadcasted_iota(jnp.int32, (8, BLK), 1)
        inside = (lane8 >= first) & (lane8 < last)
        for i in range(last // 8, BLK // 8):
            groups[i] = jnp.where(inside, 0.0, groups[i]) - update[8 * i : 8 * i + 8, :]
    return jnp.concatenate(out, axis=0)


def chan_pack_kernel(chans, blocks, rows, int_ref, map_ref, *rest):
    outs, (held, start, sem_in, sem) = rest[:chans], rest[chans:]
    load = pltpu.make_async_copy(map_ref, held.at[:, : blocks * BLK], sem_in)
    load.start()
    held[:, blocks * BLK :] = jnp.zeros((rows, BLK), F32)
    total = jnp.int32(0)
    for c in range(chans):
        start[c] = total
        total = total + int_ref[2 + blocks + c]
    load.wait()
    for p in list(range(1, chans)) + [0]:
        owner = int_ref[0] ^ p
        offset = start[owner]
        live = int_ref[2 + blocks + owner]
        for j in range(CAP):
            place = jnp.minimum(offset + j, blocks - 1)
            block = jnp.where(j < live, int_ref[2 + place], blocks)
            pltpu.make_async_copy(
                held.at[:, pl.ds(pl.multiple_of(block * BLK, BLK), BLK)],
                outs[p].at[:, j * BLK : (j + 1) * BLK],
                sem.at[p],
            ).start()
    for p in range(chans):
        pltpu.make_async_copy(held.at[:, : CAP * BLK], outs[p], sem.at[p]).wait()


def sky_pack_start(sizes, int_ref, map_ref, outs, held, table, seen, sem_in, sem):
    chans, skies, cap, rows, blocks, _ = sizes
    load = pltpu.make_async_copy(map_ref, held.at[:, : blocks * BLK], sem_in)
    load.start()
    held[:, blocks * BLK :] = jnp.zeros((rows, BLK), F32)
    width = chans * cap
    dests = 2 + blocks + chans

    def clear(i, carry):
        table[i] = blocks
        return carry

    lax.fori_loop(0, skies * width, clear, 0)

    def owner(c, offset):
        live = int_ref[2 + blocks + c]
        for d in range(skies):
            seen[d] = 0

        def slot(j, carry):
            d = int_ref[dests + c * CAP + j]
            r = seen[d]
            seen[d] = r + 1
            table[d * width + c * cap + r] = int_ref[2 + offset + j]
            return carry

        lax.fori_loop(0, live, slot, 0)
        return offset + live

    lax.fori_loop(0, chans, owner, jnp.int32(0))
    load.wait()
    for q in range(skies):
        base = (int_ref[1] ^ q) * width

        def send(i, carry, q=q, base=base):
            pltpu.make_async_copy(
                held.at[:, pl.ds(pl.multiple_of(table[base + i] * BLK, BLK), BLK)],
                outs[q].at[:, pl.ds(pl.multiple_of(i * BLK, BLK), BLK)],
                sem.at[q],
            ).start()
            return carry

        lax.fori_loop(0, width, send, 0)
    return [pltpu.make_async_copy(held.at[:, : width * BLK], outs[q], sem.at[q]) for q in range(skies)]


def eliminate_kernel(before, parts, last, merge, sources, sizes, *refs):
    chans, skies, cap, rows, blocks, nt = sizes
    refs = list(refs)
    take = lambda n: [refs.pop(0) for _ in range(n)]
    (int_ref,) = take(1)
    if before:
        (aux_ref,) = take(1)
    else:
        template_ref, noise_ref, map_ref = take(3)
    x_refs = take(len(sources))
    u_refs = take(before)
    sum_ref = take(1)[0] if before else None
    if last:
        amp_refs = take(skies)
    else:
        u_out, sum_out = take(2)
    if not before:
        (aux_ref,) = take(1)
        sky_out = take(skies)
    (xs,) = take(1)
    if last:
        (amp_scratch,) = take(1)
    wide = CAP * BLK
    size = parts * STEP
    packs = [] if before else sky_pack_start(sizes, int_ref, map_ref, sky_out, *refs)
    if not before:
        for at in range(0, aux_ref.shape[0], BLK):
            tall = jnp.concatenate(
                [
                    template_ref[:, at : at + BLK],
                    jnp.zeros((TPAD - nt, BLK), F32),
                    jnp.broadcast_to(noise_ref[:, at : at + BLK], (BLK - TPAD, BLK)),
                ],
                axis=0,
            )
            aux_ref[at : at + BLK, :] = tall.T
    for i, p in enumerate(sources):
        first = pl.multiple_of((int_ref[0] ^ p) * rows, rows)
        xs[i * rows : (i + 1) * rows, :wide] = x_refs[i][...]
        xs[i * rows : (i + 1) * rows, wide:] = aux_ref[pl.ds(first, rows), :]
    live = int_ref[2 + blocks + int_ref[0]]
    scale = 1.0 / jnp.full((1, BLK), (live * BLK).astype(F32))[:, :1]
    x = xs[:, :wide]
    row = lax.broadcasted_iota(jnp.int32, (size, size), 0)
    lane = lax.broadcasted_iota(jnp.int32, (size, size), 1)
    noise = xs[:, wide + TPAD : wide + TPAD + 1]
    s = dot(x, x, ((1,), (1,))) * scale + jnp.where(row == lane, noise, 0.0)
    lower = []
    for ref in u_refs:
        part = dot(x, ref[:, :wide], ((1,), (1,))) * scale
        s = s - dot(part, part, ((1,), (1,)))
        lower.append(part)
    value = xs[...]
    for part, ref in zip(lower, u_refs):
        value = value - dot(part, ref[...], ((1,), (0,)))
    r = inverse_factor(s[:STEP, :STEP])
    u = dot(r, value[:STEP], ((1,), (0,)))
    if parts == 2:
        side = dot(s[STEP:, :STEP], r, ((1,), (1,)))
        r2 = inverse_factor(s[STEP:, STEP:] - dot(side, side, ((1,), (1,))))
        u2 = dot(r2, value[STEP:] - dot(side, u, ((1,), (0,))), ((1,), (0,)))
        u = jnp.concatenate([u, u2], axis=0)
    part = dot(u[:, wide : wide + TPAD], u, ((0,), (0,)))
    if before:
        part = part + sum_ref[...]
    if not last:
        if merge:
            u_out[: STEP] = u_refs[0][...]
            u_out[STEP:] = u
        else:
            u_out[...] = u
        sum_out[...] = part
        for pack in packs:
            pack.wait()
        return
    row = lax.broadcasted_iota(jnp.int32, (TPAD, BLK), 0)
    lane = lax.broadcasted_iota(jnp.int32, (TPAD, BLK), 1)
    gram = jnp.where(lane < TPAD, part[:, wide:], 0.0)
    gram = gram + jnp.where((row == lane) & (row >= nt), 1.0, 0.0)
    root = panel_factor([gram[8 * g : 8 * g + 8, :] for g in range(TPAD // 8)], 0)
    root = jnp.where(lane <= row, root, 0.0)[:, :TPAD]
    amp = dot(root, dot(root, part[:, :wide], ((1,), (0,))), ((0,), (0,)))
    amp_scratch[:, :wide] = amp
    amp_scratch[:, wide:] = jnp.zeros((TPAD, BLK), F32)
    dests = 2 + blocks + chans + int_ref[0] * CAP
    for q in range(skies):
        d = int_ref[1] ^ q
        ranks = jnp.int32(0)
        slots = [jnp.int32(CAP)] * cap
        for j in range(CAP):
            here = (int_ref[dests + j] == d) & (j < live)
            for rank in range(cap):
                slots[rank] = jnp.where(here & (ranks == rank), j, slots[rank])
            ranks = ranks + here.astype(jnp.int32)
        for rank in range(cap):
            at = pl.multiple_of(slots[rank] * BLK, BLK)
            amp_refs[q][:, rank * BLK : (rank + 1) * BLK] = amp_scratch[:, pl.ds(at, BLK)]


def clean_kernel(chans, skies, cap, rows, int_ref, aux_ref, *rest):
    raws, amps = rest[:skies], rest[skies : skies + chans]
    out_ref, raw_scratch, out_scratch, sem, out_sem = rest[skies + chans :]
    width = chans * cap
    copies = []
    for q in range(skies):
        copy = pltpu.make_async_copy(raws[q], raw_scratch.at[q], sem.at[q])
        copy.start()
        copies.append(copy)
    first = pl.multiple_of(int_ref[0] * rows, rows)
    high, middle, low = split(aux_ref[pl.ds(first, rows), :][:, :TPAD])
    left = jnp.concatenate([high, high, middle, middle, high, low], axis=1)
    stores = []
    for q in range(skies):
        s = int_ref[1] ^ q
        copies[q].wait()
        for p in range(chans):
            owner = int_ref[0] ^ p
            high, middle, low = split(amps[p][q])
            right = jnp.concatenate([high, middle, high, middle, low, high], axis=0)
            model = jnp.dot(left, right, preferred_element_type=F32)
            for r in range(cap):
                slot = owner * cap + r
                at = pl.multiple_of(slot * BLK, BLK)
                value = raw_scratch[q, :, pl.ds(at, BLK)] - model[:, r * BLK : (r + 1) * BLK]
                out_scratch[q, pl.ds(slot, rows, stride=width), :] = value
        store = pltpu.make_async_copy(
            out_scratch.at[q].reshape(rows, width, BLK),
            out_ref.at[:, pl.ds(pl.multiple_of(s * width, width), width), :],
            out_sem.at[q],
        )
        store.start()
        stores.append(store)
    for store in stores:
        store.wait()


def swap(value, axis, bits):
    size = lax.axis_size(axis)
    return lax.ppermute(value, axis, [(i, i ^ bits) for i in range(size)])


def share(value, chans):
    known = {0: value}
    known[1] = swap(value, "chan", 1)
    bit = chans // 2
    while bit > 1:
        for p in sorted(k for k in known if k % 2 == 0):
            known[p ^ bit] = swap(known[p], "chan", bit)
        bit //= 2
    for p in sorted(k for k in known if k % 2 == 0 and k):
        known[p ^ 1] = swap(known[p], "chan", 1)
    return [known[p] for p in range(chans)]


def on_device(sky_map, templates, noise_var, block_order, patch_count, slab_dest):
    chans = lax.axis_size("chan")
    skies = lax.axis_size("sky")
    rows = sky_map.shape[0]
    nu, nt = templates.shape
    blocks = block_order.shape[1]
    cap = (CAP + skies - 1) // skies
    wide = CAP * BLK
    sizes = (chans, skies, cap, rows, blocks, nt)
    place = jnp.stack([lax.axis_index("chan"), lax.axis_index("sky")]).astype(jnp.int32)
    ints = jnp.concatenate([place, block_order[0], patch_count[0], slab_dest[0].reshape(-1)])

    packed = pl.pallas_call(
        functools.partial(chan_pack_kernel, chans, blocks, rows),
        out_shape=[jax.ShapeDtypeStruct((rows, wide), F32)] * chans,
        in_specs=[SMEM, HBM],
        out_specs=[HBM] * chans,
        scratch_shapes=[
            pltpu.VMEM((rows, (blocks + 1) * BLK), F32),
            pltpu.SMEM((chans,), jnp.int32),
            pltpu.SemaphoreType.DMA,
            pltpu.SemaphoreType.DMA((chans,)),
        ],
        compiler_params=PARAMS,
        name="chan_pack",
    )(ints, sky_map)
    arrived = {0: packed[0]}

    def fetch(block, after):
        for p in range(block * per_step, (block + 1) * per_step):
            if p:
                parcel = packed[p] if after is None else lax.optimization_barrier((packed[p], after))[0]
                arrived[p] = swap(parcel, "chan", p)

    per_step = STEP // rows
    steps = nu // STEP
    groups = [[0], [1]] + [[i, i + 1] for i in range(2, steps, 2)]
    starts = {-1: list(range(steps))}
    sky_starts = {1: list(range(1, skies))}
    for block in starts[-1]:
        fetch(block, None)
    held = []
    before = []
    for turn, group in enumerate(groups):
        parts = len(group)
        done = sum(before)
        sources = [p for block in group for p in range(block * per_step, (block + 1) * per_step)]
        last = done + parts == steps
        if last:
            for q in range(1, skies):
                total, raws[q] = lax.optimization_barrier((total, raws[q]))
        size = parts * STEP
        merge = turn == 1
        if last:
            out_shape = [jax.ShapeDtypeStruct((TPAD, cap * BLK), F32)] * skies
        else:
            out_shape = [
                jax.ShapeDtypeStruct((size + merge * STEP, wide + BLK), F32),
                jax.ShapeDtypeStruct((TPAD, wide + BLK), F32),
            ]
            if not before:
                out_shape.append(jax.ShapeDtypeStruct((nu, BLK), F32))
                out_shape += [jax.ShapeDtypeStruct((rows, chans * cap * BLK), F32)] * skies
        scratch = [
            pltpu.VMEM((size, wide + BLK), F32),
        ]
        if last:
            scratch.append(pltpu.VMEM((TPAD, wide + BLK), F32))
        if not before:
            scratch += [
                pltpu.VMEM((rows, (blocks + 1) * BLK), F32),
                pltpu.SMEM((skies * chans * cap,), jnp.int32),
                pltpu.SMEM((skies,), jnp.int32),
                pltpu.SemaphoreType.DMA,
                pltpu.SemaphoreType.DMA((skies,)),
            ]
        result = pl.pallas_call(
            functools.partial(eliminate_kernel, len(held), parts, last, merge, sources, sizes),
            out_shape=out_shape,
            in_specs=[SMEM]
            + ([VMEM] if before else [VMEM, VMEM, HBM])
            + [VMEM] * (len(sources) + len(held) + bool(before)),
            out_specs=[VMEM] * (len(out_shape) if before else 3) + [HBM] * (0 if before else len(out_shape) - 3),
            scratch_shapes=scratch,
            compiler_params=PARAMS,
            cost_estimate=pl.CostEstimate(
                flops=12 * size * STEP * wide * (2 * done + 2), bytes_accessed=(done + 2) * 600000, transcendentals=0
            ),
            name=f"eliminate_{done}",
        )(
            ints,
            *([aux] if before else [templates.T, noise_var.reshape(1, nu), sky_map]),
            *[arrived[p] for p in sources],
            *held,
            *([total] if before else []),
        )
        if last:
            amps = result
            break
        if not before:
            aux = result[2]
            sky_packed = result[3:]
        held = [result[0]] if merge else held + [result[0]]
        total = result[1]
        before.append(parts)
        for block in starts.get(turn, []):
            fetch(block, total)
        if turn == 0:
            raws = {0: result[3]}
        for q in sky_starts.get(turn, []):
            if q < skies:
                raws[q] = swap(lax.optimization_barrier((sky_packed[q], total))[0], "sky", q)

    mine = jnp.stack([amps[0]] + [swap(amps[q], "sky", q) for q in range(1, skies)])
    shared = share(mine, chans)
    out_rows = skies * chans * cap
    return pl.pallas_call(
        functools.partial(clean_kernel, chans, skies, cap, rows),
        out_shape=jax.ShapeDtypeStruct((rows, out_rows, BLK), F32),
        in_specs=[SMEM, VMEM] + [HBM] * skies + [VMEM] * chans,
        out_specs=HBM,
        scratch_shapes=[
            pltpu.VMEM((skies, rows, chans * cap * BLK), F32),
            pltpu.VMEM((skies, rows * chans * cap, BLK), F32),
            pltpu.SemaphoreType.DMA((skies,)),
            pltpu.SemaphoreType.DMA((skies,)),
        ],
        compiler_params=PARAMS,
        name="clean",
    )(ints, aux, *[raws[q] for q in range(skies)], *shared)


def solution(mesh):
    return jax.shard_map(
        on_device,
        mesh=mesh,
        in_specs=(P("chan", "sky"), P(), P(), P("sky", None), P("sky", None), P("sky", None, None)),
        out_specs=P("chan", "sky", None),
        check_vma=False,
    )
```
